128 devices in a mesh: gx: 16 (over y_hi, x, core), gy: 8 (over y_lo, z).
Axes of the slice: x: 4, y: 4 (y_hi: 2, y_lo: 2; y = y_hi * 2 + y_lo), z: 4, core: 2. Of those that a mesh axis runs over, the one named last changes fastest.
Arguments:
- features: bfloat16 [128, 128, 8, 256], P('gx', 'gy'), may hold values from -6 to 6
- grad_out: bfloat16 [128, 128, 8, 256], P('gx', 'gy'), may hold values from -6 to 6
- weights: bfloat16 [27, 256, 256], replicated, may hold values from -0.078125 to 0.078125
- occupied: int32 [32, 32, 2], P('gx', 'gy'), may hold values 0 or 1
Outputs:
- grad_features: bfloat16 [128, 128, 8, 256], P('gx', 'gy')
- grad_weights: float32 [27, 256, 256], replicated
The draws below stay inside these ranges and needn't reach their ends.
All inputs are finite; a program needn't handle non-finite values. No bound on the sum of `occupied` on one device may be relied on, other than what follows from the above.
Results may differ from the reference program's by a relative error of at most 0.0049.
Values may be sent and summed in bfloat16 or wider, within the bound.
No kernel may reach another device: no remote copies, remote signals or barrier semaphores. Data moves between devices by JAX's collectives and lax.ppermute only.
A program may use at most 128 MiB of HBM per device.

```python
import jax
import jax.numpy as jnp

CH = 256
BZ = 2
VZ = 8
NBX = 32
NBY = 32
NX = 128
NY = 128


def plant(drawn, key, least, top_value):
    dims = drawn.shape
    index_at = [jax.random.randint(jax.random.fold_in(key, axis), (), 0, dims[axis]) for axis in range(len(dims))]
    drawn = drawn.at[tuple(index_at)].set(least)
    longest = dims.index(max(dims))
    index_at[longest] = (index_at[longest] + 1) % dims[longest]
    return drawn.at[tuple(index_at)].set(top_value)


def level_of(rng, extent, shards, smallest, high):
    gain, own = 1.0, jax.random.fold_in(rng, 6)
    for dim, shards_of in shards:
        heights = jnp.exp(jax.random.uniform(jax.random.fold_in(own, dim), (shards_of,), jnp.float32, smallest / len(shards), high / len(shards)))
        gain = gain * jnp.repeat(heights, extent[dim] // shards_of).reshape([-1 if axis == dim else 1 for axis in range(len(extent))])
    return gain


def centred(key, extent, spread, limit, split=(), dtype=jnp.bfloat16):
    result = jax.random.normal(key, extent, jnp.float32) * spread
    if len(split) > 0:
        result = level_of(key, extent, split, -0.22, 0.18) * result
    return jnp.clip(result, min=-limit, max=limit).astype(dtype)


def setup_inputs(seed: int = 0) -> dict:
    key_of = jax.random.split(jax.random.key(seed), 5)
    features = centred(key_of[0], (NX, NY, VZ, CH), 1.0, 6.0, ((0, 16), (1, 8)))
    grad_out = centred(key_of[1], (NX, NY, VZ, CH), 1.0, 6.0, ((0, 16), (1, 8)))
    weights = centred(key_of[2], (27, CH, CH), (27 * CH) ** -0.5, 0.078125)
    occupied = plant((jax.random.randint(key_of[3], (NBX, NBY, BZ), 0, 4) < 3).astype(jnp.int32), jax.random.fold_in(key_of[3], 1), 0, 1)
    return dict(features=features, grad_out=grad_out, weights=weights, occupied=occupied)


def offsets():
    return [(a, b, c) for a in (-1, 0, 1) for b in (-1, 0, 1) for c in (-1, 0, 1)]


def expand_mask(occupied):
    cells = jnp.repeat(jnp.repeat(jnp.repeat(occupied, 4, axis=0), 4, axis=1), 4, axis=2)
    return cells.astype(jnp.bfloat16)[..., None]


def dsilu(pre):
    sig = jax.nn.sigmoid(pre)
    return sig * (1.0 + pre * (1.0 - sig))


def reference(features, grad_out, weights, occupied):
    cellmask = expand_mask(occupied)
    masked = features * cellmask
    masked_grad = grad_out * cellmask
    sx, sy, sz, chan = masked.shape
    padded = jnp.pad(masked, ((1, 1), (1, 1), (1, 1), (0, 0)))
    pre = jnp.zeros((sx * sy * sz, chan), jnp.float32)
    for index, (ox, oy, oz) in enumerate(offsets()):
        piece = padded[1 + ox:1 + ox + sx, 1 + oy:1 + oy + sy, 1 + oz:1 + oz + sz].reshape(-1, chan)
        pre = pre + jnp.dot(piece, weights[index], preferred_element_type=jnp.float32)
    pre = pre.reshape(sx, sy, sz, chan)
    dpre = (masked_grad.astype(jnp.float32) * dsilu(pre)).astype(jnp.bfloat16)
    dpad = jnp.pad(dpre, ((1, 1), (1, 1), (1, 1), (0, 0)))
    flat = dpre.reshape(-1, chan)
    total = jnp.zeros((sx * sy * sz, chan), jnp.float32)
    grads = []
    for index, (ox, oy, oz) in enumerate(offsets()):
        piece = dpad[1 - ox:1 - ox + sx, 1 - oy:1 - oy + sy, 1 - oz:1 - oz + sz].reshape(-1, chan)
        total = total + jnp.dot(piece, weights[index].T, preferred_element_type=jnp.float32)
        source = padded[1 + ox:1 + ox + sx, 1 + oy:1 + oy + sy, 1 + oz:1 + oz + sz].reshape(-1, chan)
        grads.append(jax.lax.dot_general(source, flat, (((0,), (0,)), ((), ())), preferred_element_type=jnp.float32))
    grad_features = (total.reshape(sx, sy, sz, chan) * cellmask.astype(jnp.float32)).astype(jnp.bfloat16)
    return grad_features, jnp.stack(grads)
```

```python
import functools

import jax
import jax.numpy as jnp
from jax import lax
from jax.experimental import pallas as pl
from jax.experimental.pallas import tpu as pltpu
from jax.sharding import PartitionSpec as P

AXES = ("gx", "gy")
F32, BF16 = jnp.float32, jnp.bfloat16
COUNT = 128
STAGES = ((0, 1), (1, 2), (2, 0))


def place(index):
    gx, gy = index // 8, index % 8
    return (gx // 2) % 4, (gx // 8) * 2 + gy // 4, gy % 4, gx % 2


def index_of(x, y, z, core):
    return ((y // 2) * 8 + x * 2 + core) * 8 + (y % 2) * 4 + z


def ring_pairs(stage, step):
    pairs = []
    for i in range(COUNT):
        *at, core = place(i)
        axis = STAGES[stage][core]
        at[axis] = (at[axis] + step) % 4
        pairs.append((i, index_of(*at, core)))
    return pairs


def core_pairs():
    return [(i, index_of(*place(i)[:3], 1 - place(i)[3])) for i in range(COUNT)]


def send(array, pairs):
    return lax.ppermute(array, AXES, pairs)


def where_am_i():
    gx, gy = lax.axis_index("gx"), lax.axis_index("gy")
    core = gx % 2
    at = jnp.stack([(gx // 2) % 4, (gx // 8) * 2 + gy // 4, gy % 4])
    mine = jnp.where(core == 0, at[STAGES[0][0]], at[STAGES[0][1]])
    other = jnp.where(core == 0, at[STAGES[0][1]], at[STAGES[0][0]])
    return jnp.stack([core, mine, other]).astype(jnp.int32)


def with_halo(cells, sides):
    for axis, dim in sides:
        count = lax.axis_size(axis)
        ends = count - 1
        head = lax.slice_in_dim(cells, 0, 1, axis=dim)
        tail = lax.slice_in_dim(cells, cells.shape[dim] - 1, cells.shape[dim], axis=dim)
        cells = jnp.concatenate(
            [
                lax.ppermute(tail, axis, [(i, i + 1) for i in range(ends)]),
                cells,
                lax.ppermute(head, axis, [(i + 1, i) for i in range(ends)]),
            ],
            axis=dim,
        )
    return cells


def three_views(cells):
    ext = with_halo(cells, (("gy", 1), ("gx", 0)))
    rows, wide, tall, chan = ext.shape
    return jnp.stack([ext[:, i : i + wide - 2].reshape(rows, (wide - 2) * tall, chan) for i in range(3)])


def roll_cells(field, step):
    cells, chan = field.shape
    tall = field.reshape(cells // 8, 8, chan)
    level = lax.broadcasted_iota(jnp.int32, tall.shape, 1)
    moved = pltpu.roll(tall, step % 8, 1)
    kept = jnp.where((level >= step) & (level < 8 + step), moved, 0.0)
    return kept.reshape(cells, chan)


def dsilu(pre):
    sig = jax.nn.sigmoid(pre)
    return sig * (1.0 + pre * (1.0 - sig))


def grads_kernel(at_ref, views, weights, mgrad, dpre, away, keep, shifted, turned):
    tile, chan = 256, 256
    lines = tile // 128

    for side in range(3):
        @pl.loop(0, 10)
        def _(row):
            turned[side, :, pl.ds(pl.multiple_of(row * 128, 128), 128)] = views[side, row].T

    @pl.loop(0, 8 // lines)
    def _(step):
        first = step * lines
        pieces = []
        for ox in range(3):
            for oy in range(3):
                pieces.append(views[oy, pl.ds(first + ox, lines)].reshape(tile, chan))
        left = jnp.concatenate(pieces, axis=1)
        pre = jnp.zeros((tile, chan), F32)
        for oz in range(3):
            part = jnp.dot(left, weights[:, oz].reshape(9 * chan, chan), preferred_element_type=F32)
            pre = pre + (part if oz == 1 else roll_cells(part, 1 - oz))
        here = pl.ds(pl.multiple_of(first * 128, tile), tile)
        value = (mgrad[here, :].astype(F32) * dsilu(pre)).astype(BF16)
        dpre[here, :] = value
        wide = value.astype(F32)
        shifted[here, 0:chan] = roll_cells(wide, -1).astype(BF16)
        shifted[here, chan : 2 * chan] = value
        shifted[here, 2 * chan : 3 * chan] = roll_cells(wide, 1).astype(BF16)

    core, mine, other = at_ref[0], at_ref[1], at_ref[2]

    for ox in range(3):
        @pl.loop(0, 3)
        def _(oy):
            rows = []
            for half, pos in ((core, mine), (1 - core, other)):
                for d in range(4):
                    start = pl.multiple_of(half * 128 + ((pos + d) & 3) * 32, 32)
                    rows.append(turned[oy, pl.ds(start, 32), ox * 128 : ox * 128 + 1024])
            left = jnp.concatenate(rows, axis=0)
            for oz in range(3):
                part = jnp.dot(left, shifted[:, oz * chan : (oz + 1) * chan], preferred_element_type=F32)
                keep[:, ox * 9 + oy * 3 + oz] = part[:128].reshape(4, 32, chan)
                away[:, ox * 9 + oy * 3 + oz] = part[128:].reshape(4, 32, chan).astype(BF16)


def input_kernel(views, weights, mask, out):
    tile, chan = 256, 256
    lines = tile // 128

    @pl.loop(0, 8 // lines)
    def _(step):
        first = step * lines
        pieces = []
        for ox in range(3):
            for oy in range(3):
                pieces.append(views[2 - oy, pl.ds(first + 2 - ox, lines)].reshape(tile, chan))
        left = jnp.concatenate(pieces, axis=1)
        total = jnp.zeros((tile, chan), F32)
        for oz in range(3):
            right = jnp.concatenate([weights[k, oz] for k in range(9)], axis=1)
            part = lax.dot_general(left, right, (((1,), (1,)), ((), ())), preferred_element_type=F32)
            total = total + (part if oz == 1 else roll_cells(part, oz - 1))
        here = pl.ds(pl.multiple_of(first * 128, tile), tile)
        out[here, :] = (total * mask[here, :]).astype(BF16)


def place_kernel(at_ref, *refs):
    pieces, out = refs[:8], refs[8]
    core, mine, other = at_ref[0], at_ref[1], at_ref[2]
    for d in range(4):
        for half, pos, piece in ((core, mine, pieces[d]), (1 - core, other, pieces[4 + d])):
            start = pl.multiple_of(half * 128 + ((pos - d) & 3) * 32, 32)
            out[:, pl.ds(start, 32), :] = piece[...].astype(F32)


VMEM = pl.BlockSpec(memory_space=pltpu.VMEM)
SMEM = pl.BlockSpec(memory_space=pltpu.SMEM)
PARAMS = dict(vmem_limit_bytes=36 * 2**20)


def local_grads(at, views, weights, mgrad):
    return pl.pallas_call(
        grads_kernel,
        out_shape=(
            jax.ShapeDtypeStruct((1024, 256), BF16),
            jax.ShapeDtypeStruct((4, 27, 32, 256), BF16),
            jax.ShapeDtypeStruct((4, 27, 32, 256), F32),
        ),
        in_specs=[SMEM, VMEM, VMEM, VMEM],
        out_specs=(VMEM, VMEM, VMEM),
        scratch_shapes=[pltpu.VMEM((1024, 768), BF16), pltpu.VMEM((3, 256, 1280), BF16)],
        compiler_params=pltpu.CompilerParams(**PARAMS),
        cost_estimate=pl.CostEstimate(flops=7_247_757_312, bytes_accessed=12_000_000, transcendentals=262144),
    )(at, views, weights, mgrad)


def input_grads(views, weights, mask):
    return pl.pallas_call(
        input_kernel,
        out_shape=jax.ShapeDtypeStruct((1024, 256), BF16),
        in_specs=[VMEM, VMEM, VMEM],
        out_specs=VMEM,
        compiler_params=pltpu.CompilerParams(**PARAMS),
        cost_estimate=pl.CostEstimate(flops=3_623_878_656, bytes_accessed=6_000_000, transcendentals=0),
    )(views, weights, mask)


def put_together(at, pieces):
    whole = pl.BlockSpec((9, 32, 256), lambda i: (i, 0, 0))
    return pl.pallas_call(
        place_kernel,
        grid=(3,),
        out_shape=jax.ShapeDtypeStruct((27, 256, 256), F32),
        in_specs=[SMEM] + [whole] * 8,
        out_specs=pl.BlockSpec((9, 256, 256), lambda i: (i, 0, 0)),
        compiler_params=pltpu.CompilerParams(**PARAMS),
        cost_estimate=pl.CostEstimate(flops=0, bytes_accessed=11_000_000, transcendentals=0),
    )(at, *pieces)


def from_ring(own, stage):
    one, two, three = (send(own, ring_pairs(stage, step)).astype(F32) for step in (1, 2, 3))
    return ((own.astype(F32) + two) + (one + three)).astype(BF16)


def all_sum(at, away, keep):
    both = keep + send(away, core_pairs()).astype(F32)
    got = [send(both[step].astype(BF16), ring_pairs(0, step)).astype(F32) for step in (1, 2, 3)]
    own = (both[0] + got[0] + got[1] + got[2]).astype(BF16)
    own = from_ring(own, 1)
    own = from_ring(own, 2)
    mine = [own] + [send(own, ring_pairs(0, step)) for step in (1, 2, 3)]
    other = [send(piece, core_pairs()) for piece in mine]
    return put_together(at, mine + other)


def local(features, grad_out, weights, occupied):
    at = where_am_i()
    cells = jnp.repeat(jnp.repeat(jnp.repeat(occupied, 4, axis=0), 4, axis=1), 4, axis=2)
    cellmask = cells.astype(BF16)[..., None]
    sx, sy, sz, chan = features.shape
    masked = features * cellmask
    mgrad = (grad_out * cellmask).reshape(-1, chan)
    packed = weights.reshape(9, 3, chan, chan)
    dpre, away, keep = local_grads(at, three_views(masked), packed, mgrad)
    grad_weights = all_sum(at, away, keep)
    mask = cells.astype(F32).reshape(-1, 1)
    grad_features = input_grads(three_views(dpre.reshape(masked.shape)), packed, mask)
    return grad_features.reshape(features.shape), grad_weights


def solution(mesh):
    return jax.shard_map(
        local,
        mesh=mesh,
        in_specs=(P("gx", "gy", None, None), P("gx", "gy", None, None), P(), P("gx", "gy", None)),
        out_specs=(P("gx", "gy", None, None), P()),
        check_vma=False,
    )
```

```python
import functools

import jax
import jax.numpy as jnp
from jax import lax
from jax.experimental import pallas as pl
from jax.experimental.pallas import tpu as pltpu
from jax.sharding import PartitionSpec as P

AXES = ("gx", "gy")
F32, BF16 = jnp.float32, jnp.bfloat16
COUNT = 128
ORDERS = tuple(
    tuple(tuple((first + step) % 6 for step in range(6)) for first in firsts) for firsts in ((0, 1), (3, 4))
)
GROUPS = (5, 4)


def place(index):
    gx, gy = index // 8, index % 8
    return (gx // 2) % 4, (gx // 8) * 2 + gy // 4, gy % 4, gx % 2


def index_of(x, y, z, core):
    return ((y // 2) * 8 + x * 2 + core) * 8 + (y % 2) * 4 + z


def step_pairs(chain, step):
    pairs = []
    for i in range(COUNT):
        *at, core = place(i)
        dim = ORDERS[chain][core][step]
        at[dim % 3] = at[dim % 3] ^ 1 if dim < 3 else 3 - at[dim % 3]
        pairs.append((i, index_of(*at, core)))
    return pairs


def core_pairs():
    return [(i, index_of(*place(i)[:3], 1 - place(i)[3])) for i in range(COUNT)]


def send(array, pairs):
    return lax.ppermute(array, AXES, pairs)


def where_am_i():
    gx, gy = lax.axis_index("gx"), lax.axis_index("gy")
    core = gx % 2
    at = [(gx // 2) % 4, (gx // 8) * 2 + gy // 4, gy % 4]
    side = [(v % 2) ^ (v // 2) for v in at] + [v // 2 for v in at]
    found = [core]
    for chain in range(2):
        quarters = [side[order[0]] * 2 + side[order[1]] for order in ORDERS[chain]]
        found.append(jnp.where(core == 0, quarters[0], quarters[1]))
        found.append(jnp.where(core == 0, quarters[1], quarters[0]))
    return jnp.stack(found).astype(jnp.int32)


def pair_swap(axis, first, array):
    count = lax.axis_size(axis)
    pairs = [(i, i + 1) for i in range(first, count - 1, 2)]
    return lax.ppermute(array, axis, pairs + [(b, a) for a, b in pairs])


def neighbours(axis, head, tail):
    even = lax.axis_index(axis) % 2 == 0
    one = pair_swap(axis, 0, jnp.where(even, tail, head))
    two = pair_swap(axis, 1, jnp.where(even, head, tail))
    return jnp.where(even, two, one), jnp.where(even, one, two)


def slabs(masked, mgrad, before, after):
    beside = [(b, a) for b, a in zip(before.reshape(3, 8, 8, 256), after.reshape(3, 8, 8, 256))]
    found = []
    for near, next_one in ((0, 1), (7, 6)):
        parts = []
        for line in (near, next_one):
            at = slice(line * 128, line * 128 + 128)
            parts += [beside[1][0][line], beside[0][0][line], masked[at], beside[0][1][line], beside[1][1][line]]
        at = slice(near * 128, near * 128 + 128)
        parts += [beside[2][0][near], mgrad[at], beside[2][1][near]]
        found.append(jnp.concatenate(parts))
    return found


def roll_cells(field, step):
    cells, chan = field.shape
    tall = field.reshape(cells // 8, 8, chan)
    level = lax.broadcasted_iota(jnp.int32, tall.shape, 1)
    moved = pltpu.roll(tall, step % 8, 1)
    kept = jnp.where((level >= step) & (level < 8 + step), moved, 0.0)
    return kept.reshape(cells, chan)


def dsilu(pre):
    sig = jax.nn.sigmoid(pre)
    return sig * (1.0 + pre * (1.0 - sig))


def brick_mask(occupied, bx, by):
    level = lax.broadcasted_iota(jnp.int32, (8, 256), 0)
    return jnp.where(level < 4, occupied[bx, 0, by], occupied[bx, 1, by]).astype(F32)


def line_mask(occupied, bx):
    return jnp.concatenate([brick_mask(occupied, bx, by) for by in range(4) for _ in range(4)], axis=0)


def mask_kernel(occupied, features_hbm, grad_out_hbm, masked, mgrad, head, tail, features, grad_out, arrived):
    copies = [
        pltpu.make_async_copy(features_hbm, features, arrived.at[0]),
        pltpu.make_async_copy(grad_out_hbm, grad_out, arrived.at[1]),
    ]
    for copy in copies:
        copy.start()
    masks = [line_mask(occupied, bx) for bx in range(2)]
    for copy in copies:
        copy.wait()
    for bx in range(2):
        mask = masks[bx]
        for pair in range(2):
            heads, tails = [], []
            for line in (bx * 4 + pair * 2, bx * 4 + pair * 2 + 1):
                here = slice(line * 128, line * 128 + 128)
                value = features[here, :].astype(F32) * mask
                masked[here, :] = value.astype(BF16)
                grad = grad_out[here, :].astype(F32) * mask
                mgrad[here, :] = grad.astype(BF16)
                heads.append((value[:8], value[8:16], grad[:8]))
                tails.append((value[120:], value[112:120], grad[120:]))
            for kind in range(3):
                two = slice(kind * 64 + bx * 32 + pair * 16, kind * 64 + bx * 32 + pair * 16 + 16)
                head[two, :] = jnp.concatenate([h[kind] for h in heads], axis=0).astype(BF16)
                tail[two, :] = jnp.concatenate([t[kind] for t in tails], axis=0).astype(BF16)


def levels(left, weights, oy_list, ox_list):
    pre = None
    for oz in range(3):
        right = jnp.concatenate([weights[ox * 3 + oy, oz] for ox in ox_list for oy in oy_list], axis=0)
        part = jnp.dot(left, right, preferred_element_type=F32)
        part = part if oz == 1 else roll_cells(part, 1 - oz)
        pre = part if pre is None else pre + part
    return pre


def middle_kernel(masked, weights, pre, turned, held, padded, copied):
    copy = pltpu.make_async_copy(weights, held, copied)
    copy.start()
    padded[0] = jnp.zeros((128, 256), BF16)
    padded[9] = jnp.zeros((128, 256), BF16)
    for line in range(8):
        here = slice(line * 128, line * 128 + 128)
        value = masked[here, :]
        padded[1 + line] = value
        turned[:, here] = value.T

    @pl.loop(0, 4)
    def _(step):
        pieces = [padded[pl.ds(step * 2 + ox, 2)].reshape(256, 256) for ox in range(3)]
        here = pl.ds(pl.multiple_of(step * 256, 256), 256)
        pre[here, :] = levels(jnp.concatenate(pieces, axis=1), weights, (1,), (0, 1, 2))

    copy.wait()


def sides_kernel(masked, before, after, weights, pre_in, pre, turned, held, padded, copied):
    copy = pltpu.make_async_copy(weights, held, copied)
    copy.start()
    for side in range(2):
        padded[side, 0] = jnp.zeros((128, 256), BF16)
        padded[side, 9] = jnp.zeros((128, 256), BF16)
    for pair in range(4):
        left = before[pair * 16 : pair * 16 + 16, :].astype(F32)
        right = after[pair * 16 : pair * 16 + 16, :].astype(F32)
        for i in range(2):
            line = pair * 2 + i
            here = slice(line * 128, line * 128 + 128)
            value = masked[here, :].astype(F32)
            low = jnp.concatenate([left[i * 8 : i * 8 + 8], value[:120]], axis=0).astype(BF16)
            high = jnp.concatenate([value[8:], right[i * 8 : i * 8 + 8]], axis=0).astype(BF16)
            padded[0, 1 + line] = low
            padded[1, 1 + line] = high
            turned[0, :, here] = low.T
            turned[1, :, here] = high.T

    @pl.loop(0, 4)
    def _(step):
        pieces = [padded[side, pl.ds(step * 2 + ox, 2)].reshape(256, 256) for ox in range(3) for side in range(2)]
        here = pl.ds(pl.multiple_of(step * 256, 256), 256)
        pre[here, :] = pre_in[here, :] + levels(jnp.concatenate(pieces, axis=1), weights, (0, 2), (0, 1, 2))

    copy.wait()


def chain_grads(at_ref, middle, sides, ends, shifted, away, keep, chain):
    chan = 256
    core, mine, other = at_ref[0], at_ref[1 + 2 * chain], at_ref[2 + 2 * chain]
    first = sum(GROUPS[:chain])
    for group in range(GROUPS[chain]):
        ox, oy = (first + group) // 3, (first + group) % 3
        rows = []
        for half, quarter in ((core, mine), (1 - core, other)):
            for slot in range(4):
                here = pl.ds(pl.multiple_of(half * 128 + (quarter ^ slot) * 32, 32), 32)
                cells = (lambda a, b: middle[here, a:b]) if oy == 1 else (lambda a, b: sides[oy // 2, here, a:b])
                if ox == 0:
                    row = jnp.concatenate([ends[0, oy, here, :], cells(0, 896)], axis=1)
                elif ox == 1:
                    row = cells(0, 1024)
                else:
                    row = jnp.concatenate([cells(128, 1024), ends[1, oy, here, :]], axis=1)
                rows.append(row)
        left = jnp.concatenate(rows, axis=0)
        for oz in range(3):
            part = jnp.dot(left, shifted[:, oz * chan : (oz + 1) * chan], preferred_element_type=F32)
            keep[:, :, group * 3 + oz] = part[:128].reshape(2, 2, 32, chan)
            away[:, :, group * 3 + oz] = part[128:].reshape(2, 2, 32, chan).astype(BF16)


def grads_kernel(at_ref, first, last, weights, pre, mgrad, middle, sides, dpre, shifted, ends, away, keep):
    chan = 256
    lines = []
    for end, slab in ((0, first), (1, last)):
        line = slab[0:160, :].astype(F32)
        lines.append([line[8 + oy * 8 : 136 + oy * 8].astype(BF16) for oy in range(3)])
        for oy in range(3):
            ends[end, oy] = lines[end][oy].T
    for line in range(8):
        here = slice(line * 128, line * 128 + 128)
        value = pre[here, :]
        if line in (0, 7):
            end, ox = (0, 0) if line == 0 else (1, 2)
            value = value + levels(jnp.concatenate(lines[end], axis=1), weights, (0, 1, 2), (ox,))
        value = (mgrad[here, :].astype(F32) * dsilu(value)).astype(BF16)
        dpre[here, :] = value
        wide = value.astype(F32)
        shifted[here, 0:chan] = roll_cells(wide, -1).astype(BF16)
        shifted[here, chan : 2 * chan] = value
        shifted[here, 2 * chan : 3 * chan] = roll_cells(wide, 1).astype(BF16)
    chain_grads(at_ref, middle, sides, ends, shifted, away, keep, 0)


def more_kernel(at_ref, middle, sides, ends, shifted, away, keep):
    chain_grads(at_ref, middle, sides, ends, shifted, away, keep, 1)


def border_kernel(masked, before, after, first, last, weights, border, left):
    def cells(ref, start, stop):
        return ref[start:stop, :].astype(F32)

    def wide(line):
        near, at = slice(line * 8, line * 8 + 8), slice(line * 128, line * 128 + 128)
        return jnp.concatenate(
            [sides[0][1][near], sides[0][0][near], masked[at, :].astype(F32), sides[1][0][near], sides[1][1][near]], axis=0
        )

    sides = [[cells(ref, kind * 64, kind * 64 + 64) for kind in range(2)] for ref in (before, after)]
    ends = [[cells(ref, 0, 160), cells(ref, 160, 320)] for ref in (first, last)]
    edges = [[masked[x * 128 + y * 112 : x * 128 + y * 112 + 16, :].astype(F32) for x in range(8)] for y in range(2)]
    edge = [
        jnp.concatenate([v[:8] for v in edges[0]], axis=0),
        jnp.concatenate([v[8:] for v in edges[1]], axis=0),
    ]

    def column(index, body):
        at = slice(index * 8, index * 8 + 8)
        return jnp.concatenate([ends[0][0][at], body, ends[1][0][at]], axis=0)

    above = (ends[0][1], ends[0][0], wide(0))
    below = (wide(7), ends[1][0], ends[1][1])
    low = (column(0, sides[0][1]), column(1, sides[0][0]), column(2, edge[0]))
    high = (column(17, edge[1]), column(18, sides[1][0]), column(19, sides[1][1]))
    for ox in range(3):
        for oy in range(3):
            parts = [above[ox][oy * 8 : oy * 8 + 144], below[ox][oy * 8 : oy * 8 + 144]]
            parts += [low[oy][ox * 8 : ox * 8 + 64], high[oy][ox * 8 : ox * 8 + 64]]
            k = (ox * 3 + oy) * 256
            left[:, k : k + 256] = jnp.concatenate(parts, axis=0).astype(BF16)
    pre = None
    for oz in range(3):
        part = jnp.dot(left[...], weights[:, oz].reshape(2304, 256), preferred_element_type=F32)
        part = part if oz == 1 else roll_cells(part, 1 - oz)
        pre = part if pre is None else pre + part
    grad = [cells(first, 320, 464), cells(last, 320, 464), cells(before, 128, 192), cells(after, 128, 192)]
    border[...] = (jnp.concatenate(grad, axis=0) * dsilu(pre)).astype(BF16)


def input_kernel(occupied, dpre, border, weights, out, views):
    tile, chan = 256, 256
    lines = tile // 128

    for line, start in ((0, 0), (9, 144)):
        value = border[start : start + 144, :].astype(F32)
        for side in range(3):
            views[side, line] = value[side * 8 : side * 8 + 128].astype(BF16)
    for pair in range(4):
        low = border[288 + pair * 16 : 304 + pair * 16, :].astype(F32)
        high = border[352 + pair * 16 : 368 + pair * 16, :].astype(F32)
        for i in range(2):
            line = pair * 2 + i
            value = dpre[line * 128 : line * 128 + 128, :]
            views[1, 1 + line] = value
            value = value.astype(F32)
            views[0, 1 + line] = jnp.concatenate([low[i * 8 : i * 8 + 8], value[:120]], axis=0).astype(BF16)
            views[2, 1 + line] = jnp.concatenate([value[8:], high[i * 8 : i * 8 + 8]], axis=0).astype(BF16)

    @pl.loop(0, 8 // lines)
    def _(step):
        first = step * lines
        pieces = []
        for ox in range(3):
            for oy in range(3):
                pieces.append(views[2 - oy, pl.ds(first + 2 - ox, lines)].reshape(tile, chan))
        left = jnp.concatenate(pieces, axis=1)
        total = None
        for oz in range(3):
            right = jnp.concatenate([weights[k, oz] for k in range(9)], axis=1)
            part = lax.dot_general(left, right, (((1,), (1,)), ((), ())), preferred_element_type=F32)
            part = part if oz == 1 else roll_cells(part, oz - 1)
            total = part if total is None else total + part
        mask = line_mask(occupied, step // 2)
        here = pl.ds(pl.multiple_of(first * 128, tile), tile)
        out[here, :] = (total * jnp.concatenate([mask, mask], axis=0)).astype(BF16)


def place_kernel(far, sides, at_ref, *refs):
    pieces, out, built, done = refs[: 2 * len(sides)], refs[-3], refs[-2], refs[-1]
    copies = []
    for chain in range(2):
        for side in sides:
            half = at_ref[0] if side == 0 else 1 - at_ref[0]
            quarter = at_ref[1 + 2 * chain + side]
            pair = (quarter // 2) ^ far
            row = pl.multiple_of(half * 128 + pair * 64, 64)
            for group in range(GROUPS[chain]):
                first = 3 * (sum(GROUPS[:chain]) + group)
                here = slice(first, first + 3)
                for slot in range(2):
                    start = pl.multiple_of(((quarter % 2) ^ slot) * 32, 32)
                    value = pieces[chain * len(sides) + side - sides[0]][slot, group * 3 : group * 3 + 3]
                    built[side - sides[0], here, pl.ds(start, 32), :] = value.astype(F32)
                copy = pltpu.make_async_copy(
                    built.at[side - sides[0], here], out.at[here, pl.ds(row, 64), :], done.at[len(copies)]
                )
                copy.start()
                copies.append(copy)
    for copy in copies:
        copy.wait()


VMEM = pl.BlockSpec(memory_space=pltpu.VMEM)
SMEM = pl.BlockSpec(memory_space=pltpu.SMEM)
HBM = pl.BlockSpec(memory_space=pltpu.HBM)


def shape(*dims, dtype=BF16):
    return jax.ShapeDtypeStruct(dims, dtype)


def chain_shapes(chain):
    dims = (2, 2, 3 * GROUPS[chain], 32, 256)
    return shape(*dims), shape(*dims, dtype=F32)


def kernel(body, outs, specs, args, flops, scratch=(), out_specs=None, aliases=None, nbytes=6_000_000, room=20):
    return pl.pallas_call(
        body,
        out_shape=outs,
        in_specs=specs,
        out_specs=out_specs if out_specs is not None else jax.tree.map(lambda _: VMEM, outs),
        scratch_shapes=scratch,
        input_output_aliases=aliases or {},
        compiler_params=pltpu.CompilerParams(vmem_limit_bytes=room * 2**20),
        cost_estimate=pl.CostEstimate(flops=flops, bytes_accessed=nbytes, transcendentals=0),
    )(*args)


def put_in_place(far, sides, at, pieces, out=None):
    more = () if out is None else (out,)
    return kernel(
        functools.partial(place_kernel, far, sides),
        shape(27, 256, 256, dtype=F32),
        [SMEM] + [VMEM] * len(pieces) + [HBM] * len(more),
        (at, *pieces, *more),
        0,
        [pltpu.VMEM((len(sides), 27, 64, 256), F32), pltpu.SemaphoreType.DMA((9 * len(sides),))],
        HBM,
        {1 + len(pieces): 0} if more else {},
        nbytes=10_000_000,
    )


def halved(chain, total):
    for step in range(2):
        total = total[0] + send(total[1].astype(BF16), step_pairs(chain, step)).astype(F32)
    return total.astype(BF16)


def summed(chain, own, step):
    return (own.astype(F32) + send(own, step_pairs(chain, step)).astype(F32)).astype(BF16)


def gathered(chain, own):
    near = jnp.stack([own, send(own, step_pairs(chain, 1))])
    return near, send(near, step_pairs(chain, 0))


CONV = 3_623_878_656


def local(features, grad_out, weights, occupied):
    at = where_am_i()
    cells, chan = 1024, 256
    packed = weights.reshape(9, 3, chan, chan)
    occupied = jnp.transpose(occupied, (0, 2, 1))
    masked, mgrad, head, tail = kernel(
        mask_kernel,
        (shape(cells, chan), shape(cells, chan), shape(192, chan), shape(192, chan)),
        [SMEM, HBM, HBM],
        (occupied, features.reshape(cells, chan), grad_out.reshape(cells, chan)),
        0,
        [pltpu.VMEM((cells, chan), BF16), pltpu.VMEM((cells, chan), BF16), pltpu.SemaphoreType.DMA((2,))],
        nbytes=2_000_000,
    )
    before, after = neighbours("gy", head, tail)
    held = shape(9, 3, chan, chan)
    pre, middle, kept = kernel(
        middle_kernel,
        (shape(cells, chan, dtype=F32), shape(chan, cells), held),
        [VMEM, VMEM],
        (masked, packed),
        CONV // 3,
        [pltpu.VMEM((10, 128, chan), BF16), pltpu.SemaphoreType.DMA],
    )
    before, after, pre = lax.optimization_barrier((before, after, pre))
    first, last = neighbours("gx", *slabs(masked, mgrad, before, after))
    pre, sides, kept = kernel(
        sides_kernel,
        (shape(cells, chan, dtype=F32), shape(2, chan, cells), held),
        [VMEM] * 5,
        (masked, before, after, kept, pre),
        2 * CONV // 3,
        [pltpu.VMEM((2, 10, 128, chan), BF16), pltpu.SemaphoreType.DMA],
    )
    dpre, shifted, ends, away, keep = kernel(
        grads_kernel,
        (shape(cells, chan), shape(cells, 3 * chan), shape(2, 3, chan, 128), *chain_shapes(0)),
        [SMEM] + [VMEM] * 7,
        (at, first, last, kept, pre, mgrad, middle, sides),
        2 * CONV // 3,
    )
    got = send(away, core_pairs())
    away, more_keep = kernel(
        more_kernel, chain_shapes(1), [SMEM] + [VMEM] * 4, (at, middle, sides, ends, shifted), CONV // 2
    )
    away, got = lax.optimization_barrier((away, got))
    more_got = send(away, core_pairs())
    sums = [halved(0, keep + got.astype(F32)), halved(1, more_keep + more_got.astype(F32))]
    border = kernel(
        border_kernel,
        shape(416, chan),
        [VMEM] * 6,
        (masked, before, after, first, last, packed),
        CONV // 2,
        [pltpu.VMEM((416, 9 * chan), BF16)],
    )
    for step in range(2, 6):
        sums = [summed(chain, own, step) for chain, own in enumerate(sums)]
        if step == 3:
            sums, border = lax.optimization_barrier((sums, border))
            grad_features = kernel(
                input_kernel,
                shape(cells, chan),
                [SMEM, VMEM, VMEM, VMEM],
                (occupied, dpre, border, packed),
                CONV,
                [pltpu.VMEM((3, 10, 128, chan), BF16)],
            )
        if step == 4:
            sums, grad_features = lax.optimization_barrier((sums, grad_features))
    nears, fars = zip(*(gathered(chain, own) for chain, own in enumerate(sums)))
    pieces = [p for near in nears for p in (near, send(near, core_pairs()))]
    out = put_in_place(0, (0, 1), at, pieces)
    fars, out = lax.optimization_barrier((fars, out))
    others = [send(far, core_pairs()) for far in fars]
    out = put_in_place(1, (0,), at, fars, out)
    out = put_in_place(1, (1,), at, others, out)
    return grad_features.reshape(features.shape), out


def solution(mesh):
    return jax.shard_map(
        local,
        mesh=mesh,
        in_specs=(P("gx", "gy", None, None), P("gx", "gy", None, None), P(), P("gx", "gy", None)),
        out_specs=(P("gx", "gy", None, None), P()),
        check_vma=False,
    )
```

```python
import functools

import jax
import jax.numpy as jnp
from jax import lax
from jax.experimental import pallas as pl
from jax.experimental.pallas import tpu as pltpu
from jax.sharding import PartitionSpec as P

AXES = ("gx", "gy")
F32, BF16 = jnp.float32, jnp.bfloat16
COUNT = 128
FIRSTS = ((0, 1), (3, 4))
ORDERS = tuple(
    tuple(tuple((first + step) % 6 for step in range(6)) for first in firsts) for firsts in FIRSTS
)
GROUPS = (5, 4)
CHAINS = len(GROUPS)


def place(index):
    gx, gy = index // 8, index % 8
    return (gx // 2) % 4, (gx // 8) * 2 + gy // 4, gy % 4, gx % 2


def index_of(x, y, z, core):
    return ((y // 2) * 8 + x * 2 + core) * 8 + (y % 2) * 4 + z


def step_pairs(chain, step):
    pairs = []
    for i in range(COUNT):
        *at, core = place(i)
        dim = ORDERS[chain][core][step]
        at[dim % 3] = at[dim % 3] ^ 1 if dim < 3 else 3 - at[dim % 3]
        pairs.append((i, index_of(*at, core)))
    return pairs


def core_pairs():
    return [(i, index_of(*place(i)[:3], 1 - place(i)[3])) for i in range(COUNT)]


def send(array, pairs):
    return lax.ppermute(array, AXES, pairs)


def where_am_i():
    gx, gy = lax.axis_index("gx"), lax.axis_index("gy")
    core = gx % 2
    at = [(gx // 2) % 4, (gx // 8) * 2 + gy // 4, gy % 4]
    side = [(v % 2) ^ (v // 2) for v in at] + [v // 2 for v in at]
    found = [core]
    for chain in range(CHAINS):
        quarters = [side[order[0]] * 2 + side[order[1]] for order in ORDERS[chain]]
        found.append(jnp.where(core == 0, quarters[0], quarters[1]))
        found.append(jnp.where(core == 0, quarters[1], quarters[0]))
    return jnp.stack(found).astype(jnp.int32)


def pair_swap(axis, first, array):
    count = lax.axis_size(axis)
    pairs = [(i, i + 1) for i in range(first, count - 1, 2)]
    return lax.ppermute(array, axis, pairs + [(b, a) for a, b in pairs])


def neighbours(axis, head, tail):
    even = lax.axis_index(axis) % 2 == 0
    one = pair_swap(axis, 0, jnp.where(even, tail, head))
    two = pair_swap(axis, 1, jnp.where(even, head, tail))
    return jnp.where(even, two, one), jnp.where(even, one, two)


def slabs(masked, mgrad, before, after):
    beside = [(b, a) for b, a in zip(before.reshape(3, 8, 8, 256), after.reshape(3, 8, 8, 256))]
    found = []
    for near, next_one in ((0, 1), (7, 6)):
        parts = []
        for line in (near, next_one):
            at = slice(line * 128, line * 128 + 128)
            parts += [beside[1][0][line], beside[0][0][line], masked[at], beside[0][1][line], beside[1][1][line]]
        at = slice(near * 128, near * 128 + 128)
        parts += [beside[2][0][near], mgrad[at], beside[2][1][near]]
        found.append(jnp.concatenate(parts))
    return found


def roll_cells(field, step):
    cells, chan = field.shape
    tall = field.reshape(cells // 8, 8, chan)
    level = lax.broadcasted_iota(jnp.int32, tall.shape, 1)
    moved = pltpu.roll(tall, step % 8, 1)
    kept = jnp.where((level >= step) & (level < 8 + step), moved, 0.0)
    return kept.reshape(cells, chan)


def dsilu(pre):
    sig = jax.nn.sigmoid(pre)
    return sig * (1.0 + pre * (1.0 - sig))


def brick_mask(occupied, bx, by):
    level = lax.broadcasted_iota(jnp.int32, (8, 256), 0)
    return jnp.where(level < 4, occupied[bx, 0, by], occupied[bx, 1, by]).astype(F32)


def line_mask(occupied, bx):
    return jnp.concatenate([brick_mask(occupied, bx, by) for by in range(4) for _ in range(4)], axis=0)


def mask_kernel(occupied, mask):
    for bx in range(2):
        lines = line_mask(occupied, bx).astype(BF16)
        for line in range(bx * 4, bx * 4 + 4):
            mask[line * 128 : line * 128 + 128, :] = lines


def levels(left, weights, oy_list, ox_list):
    pre = None
    for oz in range(3):
        right = jnp.concatenate([weights[ox * 3 + oy, oz] for ox in ox_list for oy in oy_list], axis=0)
        part = jnp.dot(left, right, preferred_element_type=F32)
        part = part if oz == 1 else roll_cells(part, 1 - oz)
        pre = part if pre is None else pre + part
    return pre


def inner_kernel(masked, before, after, weights, pre, turned, held, padded, copied):
    copy = pltpu.make_async_copy(weights, held, copied)
    copy.start()
    for side in range(3):
        padded[side, 0] = jnp.zeros((128, 256), BF16)
        padded[side, 9] = jnp.zeros((128, 256), BF16)
    for pair in range(4):
        left = before[pair * 16 : pair * 16 + 16, :].astype(F32)
        right = after[pair * 16 : pair * 16 + 16, :].astype(F32)
        for i in range(2):
            line = pair * 2 + i
            here = slice(line * 128, line * 128 + 128)
            value = masked[here, :]
            wide = value.astype(F32)
            low = jnp.concatenate([left[i * 8 : i * 8 + 8], wide[:120]], axis=0).astype(BF16)
            high = jnp.concatenate([wide[8:], right[i * 8 : i * 8 + 8]], axis=0).astype(BF16)
            for side, field in enumerate((low, value, high)):
                padded[side, 1 + line] = field
                turned[side, :, here] = field.T

    @pl.loop(0, 2)
    def _(step):
        pieces = [padded[oy, pl.ds(step * 4 + ox, 4)].reshape(512, 256) for ox in range(3) for oy in range(3)]
        here = pl.ds(pl.multiple_of(step * 512, 512), 512)
        pre[here, :] = levels(jnp.concatenate(pieces, axis=1), weights, (0, 1, 2), (0, 1, 2))

    copy.wait()


def chain_grads(at_ref, turned, ends, shifted, away, keep, chain):
    chan = 256
    core, mine, other = at_ref[0], at_ref[1 + 2 * chain], at_ref[2 + 2 * chain]
    for group in range(GROUPS[chain]):
        ox, oy = divmod(sum(GROUPS[:chain]) + group, 3)
        rows = []
        for half, quarter in ((core, mine), (1 - core, other)):
            for slot in range(4):
                here = pl.ds(pl.multiple_of(half * 128 + (quarter ^ slot) * 32, 32), 32)
                if ox == 0:
                    row = jnp.concatenate([ends[0, oy, here, :], turned[oy, here, 0:896]], axis=1)
                elif ox == 1:
                    row = turned[oy, here, :]
                else:
                    row = jnp.concatenate([turned[oy, here, 128:1024], ends[1, oy, here, :]], axis=1)
                rows.append(row)
        left = jnp.concatenate(rows, axis=0)
        for oz in range(3):
            part = jnp.dot(left, shifted[:, oz * chan : (oz + 1) * chan], preferred_element_type=F32)
            keep[:, :, group * 3 + oz] = part[:128].reshape(2, 2, 32, chan)
            away[:, :, group * 3 + oz] = part[128:].reshape(2, 2, 32, chan).astype(BF16)


def grads_kernel(at_ref, first, last, weights, pre, mgrad, turned, dpre, shifted, ends, away, keep):
    chan = 256
    lines = []
    for end, slab in ((0, first), (1, last)):
        line = slab[0:160, :].astype(F32)
        lines.append([line[8 + oy * 8 : 136 + oy * 8].astype(BF16) for oy in range(3)])
        for oy in range(3):
            ends[end, oy] = lines[end][oy].T
    for line in range(8):
        here = slice(line * 128, line * 128 + 128)
        value = pre[here, :]
        if line in (0, 7):
            end, ox = (0, 0) if line == 0 else (1, 2)
            value = value + levels(jnp.concatenate(lines[end], axis=1), weights, (0, 1, 2), (ox,))
        value = (mgrad[here, :].astype(F32) * dsilu(value)).astype(BF16)
        dpre[here, :] = value
        wide = value.astype(F32)
        shifted[here, 0:chan] = roll_cells(wide, -1).astype(BF16)
        shifted[here, chan : 2 * chan] = value
        shifted[here, 2 * chan : 3 * chan] = roll_cells(wide, 1).astype(BF16)
    chain_grads(at_ref, turned, ends, shifted, away, keep, 0)


def more_kernel(chain, at_ref, turned, ends, shifted, away, keep):
    chain_grads(at_ref, turned, ends, shifted, away, keep, chain)


def border_kernel(masked, before, after, first, last, weights, border, left):
    def cells(ref, start, stop):
        return ref[start:stop, :].astype(F32)

    def wide(line):
        near, at = slice(line * 8, line * 8 + 8), slice(line * 128, line * 128 + 128)
        return jnp.concatenate(
            [sides[0][1][near], sides[0][0][near], masked[at, :].astype(F32), sides[1][0][near], sides[1][1][near]], axis=0
        )

    sides = [[cells(ref, kind * 64, kind * 64 + 64) for kind in range(2)] for ref in (before, after)]
    ends = [[cells(ref, 0, 160), cells(ref, 160, 320)] for ref in (first, last)]
    edges = [[masked[x * 128 + y * 112 : x * 128 + y * 112 + 16, :].astype(F32) for x in range(8)] for y in range(2)]
    edge = [
        jnp.concatenate([v[:8] for v in edges[0]], axis=0),
        jnp.concatenate([v[8:] for v in edges[1]], axis=0),
    ]

    def column(index, body):
        at = slice(index * 8, index * 8 + 8)
        return jnp.concatenate([ends[0][0][at], body, ends[1][0][at]], axis=0)

    above = (ends[0][1], ends[0][0], wide(0))
    below = (wide(7), ends[1][0], ends[1][1])
    low = (column(0, sides[0][1]), column(1, sides[0][0]), column(2, edge[0]))
    high = (column(17, edge[1]), column(18, sides[1][0]), column(19, sides[1][1]))
    for ox in range(3):
        for oy in range(3):
            parts = [above[ox][oy * 8 : oy * 8 + 144], below[ox][oy * 8 : oy * 8 + 144]]
            parts += [low[oy][ox * 8 : ox * 8 + 64], high[oy][ox * 8 : ox * 8 + 64]]
            k = (ox * 3 + oy) * 256
            left[:, k : k + 256] = jnp.concatenate(parts, axis=0).astype(BF16)
    pre = None
    for oz in range(3):
        part = jnp.dot(left[...], weights[:, oz].reshape(2304, 256), preferred_element_type=F32)
        part = part if oz == 1 else roll_cells(part, 1 - oz)
        pre = part if pre is None else pre + part
    grad = [cells(first, 320, 464), cells(last, 320, 464), cells(before, 128, 192), cells(after, 128, 192)]
    border[...] = (jnp.concatenate(grad, axis=0) * dsilu(pre)).astype(BF16)


def input_kernel(part, occupied, dpre, border, weights, out, views):
    tile, chan = 512, 256
    lines = tile // 128

    line, start = ((0, 0), (5, 144))[part]
    value = border[start : start + 144, :].astype(F32)
    for side in range(3):
        views[side, line] = value[side * 8 : side * 8 + 128].astype(BF16)
    for pair in range(part, part + 3):
        low = border[288 + pair * 16 : 304 + pair * 16, :].astype(F32)
        high = border[352 + pair * 16 : 368 + pair * 16, :].astype(F32)
        for i in range(2):
            line = pair * 2 + i
            slot = line + 1 - part * 4
            if not 0 <= slot <= 5:
                continue
            value = dpre[line * 128 : line * 128 + 128, :]
            views[1, slot] = value
            value = value.astype(F32)
            views[0, slot] = jnp.concatenate([low[i * 8 : i * 8 + 8], value[:120]], axis=0).astype(BF16)
            views[2, slot] = jnp.concatenate([value[8:], high[i * 8 : i * 8 + 8]], axis=0).astype(BF16)

    pieces = []
    for ox in range(3):
        for oy in range(3):
            pieces.append(views[2 - oy, 2 - ox : 6 - ox].reshape(tile, chan))
    left = jnp.concatenate(pieces, axis=1)
    total = None
    for oz in range(3):
        right = jnp.concatenate([weights[k, oz] for k in range(9)], axis=1)
        field = lax.dot_general(left, right, (((1,), (1,)), ((), ())), preferred_element_type=F32)
        field = field if oz == 1 else roll_cells(field, oz - 1)
        total = field if total is None else total + field
    out[...] = (total * jnp.concatenate([line_mask(occupied, part)] * lines, axis=0)).astype(BF16)


def place_kernel(parts, at_ref, *refs):
    pieces, out, built, done = refs[: CHAINS * len(parts)], refs[-3], refs[-2], refs[-1]
    copies = []
    for index, (far, side) in enumerate(parts):
        half = at_ref[0] if side == 0 else 1 - at_ref[0]
        for chain in range(CHAINS):
            quarter = at_ref[1 + 2 * chain + side]
            row = pl.multiple_of(half * 128 + ((quarter // 2) ^ far) * 64, 64)
            for group in range(GROUPS[chain]):
                first = 3 * (sum(GROUPS[:chain]) + group)
                here = slice(first, first + 3)
                for slot in range(2):
                    start = pl.multiple_of(((quarter % 2) ^ slot) * 32, 32)
                    value = pieces[index * CHAINS + chain][slot, group * 3 : group * 3 + 3]
                    built[index, here, pl.ds(start, 32), :] = value.astype(F32)
                copy = pltpu.make_async_copy(
                    built.at[index, here], out.at[here, pl.ds(row, 64), :], done.at[len(copies)]
                )
                copy.start()
                copies.append(copy)
    for copy in copies:
        copy.wait()


VMEM = pl.BlockSpec(memory_space=pltpu.VMEM)
SMEM = pl.BlockSpec(memory_space=pltpu.SMEM)
HBM = pl.BlockSpec(memory_space=pltpu.HBM)


def shape(*dims, dtype=BF16):
    return jax.ShapeDtypeStruct(dims, dtype)


def chain_shapes(chain):
    dims = (2, 2, 3 * GROUPS[chain], 32, 256)
    return shape(*dims), shape(*dims, dtype=F32)


def kernel(body, outs, specs, args, flops, scratch=(), out_specs=None, aliases=None, nbytes=6_000_000, room=20):
    return pl.pallas_call(
        body,
        out_shape=outs,
        in_specs=specs,
        out_specs=out_specs if out_specs is not None else jax.tree.map(lambda _: VMEM, outs),
        scratch_shapes=scratch,
        input_output_aliases=aliases or {},
        compiler_params=pltpu.CompilerParams(vmem_limit_bytes=room * 2**20),
        cost_estimate=pl.CostEstimate(flops=flops, bytes_accessed=nbytes, transcendentals=0),
    )(*args)


def put_in_place(parts, at, pieces, out=None):
    more = () if out is None else (out,)
    return kernel(
        functools.partial(place_kernel, parts),
        shape(27, 256, 256, dtype=F32),
        [SMEM] + [VMEM] * len(pieces) + [HBM] * len(more),
        (at, *pieces, *more),
        0,
        [pltpu.VMEM((len(parts), 27, 64, 256), F32), pltpu.SemaphoreType.DMA((9 * len(parts),))],
        HBM,
        {1 + len(pieces): 0} if more else {},
        nbytes=10_000_000,
    )


CONV = 3_623_878_656


def local(features, grad_out, weights, occupied):
    at = where_am_i()
    cells, chan = 1024, 256
    packed = weights.reshape(9, 3, chan, chan)
    occupied = jnp.transpose(occupied, (0, 2, 1))
    mask = kernel(mask_kernel, shape(cells, chan), [SMEM], (occupied,), 0, nbytes=500_000).reshape(features.shape)
    masked, mgrad = features * mask, grad_out * mask
    head, tail = (
        jnp.concatenate([v.reshape(64, chan) for v in (masked[:, a], masked[:, b], mgrad[:, a])]) for a, b in ((0, 1), (15, 14))
    )
    masked, mgrad = masked.reshape(cells, chan), mgrad.reshape(cells, chan)
    before, after = neighbours("gy", head, tail)
    first, last_line = neighbours("gx", *slabs(masked, mgrad, before, after))
    pre, turned, held = kernel(
        inner_kernel,
        (shape(cells, chan, dtype=F32), shape(3, chan, cells), shape(9, 3, chan, chan)),
        [VMEM] * 4,
        (masked, before, after, packed),
        CONV,
        [pltpu.VMEM((3, 10, 128, chan), BF16), pltpu.SemaphoreType.DMA],
    )
    dpre, shifted, ends, away, keep = kernel(
        grads_kernel,
        (shape(cells, chan), shape(cells, 3 * chan), shape(2, 3, chan, 128), *chain_shapes(0)),
        [SMEM] + [VMEM] * 6,
        (at, first, last_line, held, pre, mgrad, turned),
        CONV // 2,
    )
    got, keeps, tie = [], [keep], lax.optimization_barrier
    for chain in range(CHAINS):
        got.append(send(away, core_pairs()))
        if chain < CHAINS - 1:
            away, keep = kernel(
                functools.partial(more_kernel, chain + 1),
                chain_shapes(chain + 1),
                [SMEM] + [VMEM] * 3,
                (at, turned, ends, shifted),
                CONV // 3,
            )
            keeps.append(keep)
            away, got[chain] = tie((away, got[chain]))
    halves = []
    sums = [keep + g.astype(F32) for keep, g in zip(keeps, got)]
    for step in range(6):
        for chain in range(CHAINS):
            give = sums[chain][1].astype(BF16) if step < 2 else sums[chain]
            got[chain] = send(give, step_pairs(chain, step))
        if step == 3:
            border = kernel(
                border_kernel,
                shape(416, chan),
                [VMEM] * 6,
                (masked, before, after, first, last_line, packed),
                CONV // 2,
                [pltpu.VMEM((416, 9 * chan), BF16)],
            )
            got[0], border = tie((got[0], border))
        if step > 3:
            half = kernel(
                functools.partial(input_kernel, step - 4),
                shape(cells // 2, chan),
                [SMEM, VMEM, VMEM, VMEM],
                (occupied, dpre, border, packed),
                CONV // 2,
                [pltpu.VMEM((3, 6, 128, chan), BF16)],
            )
            got[0], half = tie((got[0], half))
            halves.append(half)
        for chain in range(CHAINS):
            if chain == 0 and step:
                got[0], sums[-1] = tie((got[0], sums[-1]))
            own = sums[chain][0] if step < 2 else sums[chain]
            total = own.astype(F32) + got[chain].astype(F32)
            sums[chain] = total if step < 1 else total.astype(BF16)
    for chain in range(CHAINS):
        got[chain] = send(sums[chain], step_pairs(chain, 1))
    grad_features = jnp.concatenate(halves)
    got[0], sums[-1], grad_features = tie((got[0], sums[-1], grad_features))
    nears, fars = [], []
    for chain in range(CHAINS):
        nears.append(jnp.stack([sums[chain], got[chain]]))
        fars.append(send(nears[chain], step_pairs(chain, 0)))
    out = put_in_place(((0, 0),), at, nears)
    fars[0], out, *nears = tie((fars[0], out, *nears))
    other_nears = [send(near, core_pairs()) for near in nears]
    others = [send(far, core_pairs()) for far in fars]
    out = put_in_place(((1, 0), (0, 1)), at, fars + other_nears, out)
    out = put_in_place(((1, 1),), at, others, out)
    return grad_features.reshape(features.shape), out


def solution(mesh):
    return jax.shard_map(
        local,
        mesh=mesh,
        in_specs=(P("gx", "gy", None, None), P("gx", "gy", None, None), P(), P("gx", "gy", None)),
        out_specs=(P("gx", "gy", None, None), P()),
        check_vma=False,
    )
```

```python
import functools

import jax
import jax.numpy as jnp
from jax import lax
from jax.experimental import pallas as pl
from jax.experimental.pallas import tpu as pltpu
from jax.sharding import PartitionSpec as P

AXES = ("gx", "gy")
F32, BF16 = jnp.float32, jnp.bfloat16
COUNT = 128
FIRSTS = ((0, 2), (3, 5))
ORDERS = tuple(
    tuple(tuple((first + step) % 6 for step in range(6)) for first in firsts) for firsts in FIRSTS
)
GROUPS = (5, 4)
CHAINS = len(GROUPS)


def place(index):
    gx, gy = index // 8, index % 8
    return (gx // 2) % 4, (gx // 8) * 2 + gy // 4, gy % 4, gx % 2


def index_of(x, y, z, core):
    return ((y // 2) * 8 + x * 2 + core) * 8 + (y % 2) * 4 + z


def step_pairs(chain, step):
    pairs = []
    for i in range(COUNT):
        *at, core = place(i)
        dim = ORDERS[chain][core][step]
        at[dim % 3] = at[dim % 3] ^ 1 if dim < 3 else 3 - at[dim % 3]
        pairs.append((i, index_of(*at, core)))
    return pairs


def core_pairs():
    return [(i, index_of(*place(i)[:3], 1 - place(i)[3])) for i in range(COUNT)]


def send(array, pairs):
    return lax.ppermute(array, AXES, pairs)


def where_am_i():
    gx, gy = lax.axis_index("gx"), lax.axis_index("gy")
    core = gx % 2
    at = [(gx // 2) % 4, (gx // 8) * 2 + gy // 4, gy % 4]
    side = [(v % 2) ^ (v // 2) for v in at] + [v // 2 for v in at]
    found = [core]
    for chain in range(CHAINS):
        quarters = [side[order[0]] * 2 + side[order[1]] for order in ORDERS[chain]]
        found.append(jnp.where(core == 0, quarters[0], quarters[1]))
        found.append(jnp.where(core == 0, quarters[1], quarters[0]))
    return jnp.stack(found).astype(jnp.int32)


def pair_swap(axis, first, array):
    count = lax.axis_size(axis)
    pairs = [(i, i + 1) for i in range(first, count - 1, 2)]
    return lax.ppermute(array, axis, pairs + [(b, a) for a, b in pairs])


def neighbours(axis, head, tail):
    even = lax.axis_index(axis) % 2 == 0
    one = pair_swap(axis, 0, jnp.where(even, tail, head))
    two = pair_swap(axis, 1, jnp.where(even, head, tail))
    return jnp.where(even, two, one), jnp.where(even, one, two)


def slabs(masked, mgrad, before, after):
    beside = [(b, a) for b, a in zip(before.reshape(3, 8, 8, 256), after.reshape(3, 8, 8, 256))]
    found = []
    for near, next_one in ((0, 1), (7, 6)):
        parts = []
        for line in (near, next_one):
            at = slice(line * 128, line * 128 + 128)
            parts += [beside[1][0][line], beside[0][0][line], masked[at], beside[0][1][line], beside[1][1][line]]
        at = slice(near * 128, near * 128 + 128)
        parts += [beside[2][0][near], mgrad[at], beside[2][1][near]]
        found.append(jnp.concatenate(parts))
    return found


def roll_cells(field, step):
    cells, chan = field.shape
    tall = field.reshape(cells // 8, 8, chan)
    level = lax.broadcasted_iota(jnp.int32, tall.shape, 1)
    moved = pltpu.roll(tall, step % 8, 1)
    kept = jnp.where((level >= step) & (level < 8 + step), moved, 0.0)
    return kept.reshape(cells, chan)


def dsilu(pre):
    sig = jax.nn.sigmoid(pre)
    return sig * (1.0 + pre * (1.0 - sig))


def brick_mask(occupied, bx, by):
    level = lax.broadcasted_iota(jnp.int32, (8, 256), 0)
    return jnp.where(level < 4, occupied[bx, 0, by], occupied[bx, 1, by]).astype(F32)


def line_mask(occupied, bx):
    return jnp.concatenate([brick_mask(occupied, bx, by) for by in range(4) for _ in range(4)], axis=0)


def mask_kernel(occupied, mask):
    for bx in range(2):
        lines = line_mask(occupied, bx).astype(BF16)
        for line in range(bx * 4, bx * 4 + 4):
            mask[line * 128 : line * 128 + 128, :] = lines


def levels(left, weights, oy_list, ox_list):
    pre = None
    for oz in range(3):
        right = jnp.concatenate([weights[ox * 3 + oy, oz] for ox in ox_list for oy in oy_list], axis=0)
        part = jnp.dot(left, right, preferred_element_type=F32)
        part = part if oz == 1 else roll_cells(part, 1 - oz)
        pre = part if pre is None else pre + part
    return pre


def inner_kernel(masked, before, after, weights, pre, turned, held, padded, copied):
    copy = pltpu.make_async_copy(weights, held, copied)
    copy.start()
    for side in range(3):
        padded[side, 0] = jnp.zeros((128, 256), BF16)
        padded[side, 9] = jnp.zeros((128, 256), BF16)
    for pair in range(4):
        left = before[pair * 16 : pair * 16 + 16, :].astype(F32)
        right = after[pair * 16 : pair * 16 + 16, :].astype(F32)
        for i in range(2):
            line = pair * 2 + i
            here = slice(line * 128, line * 128 + 128)
            value = masked[here, :]
            wide = value.astype(F32)
            low = jnp.concatenate([left[i * 8 : i * 8 + 8], wide[:120]], axis=0).astype(BF16)
            high = jnp.concatenate([wide[8:], right[i * 8 : i * 8 + 8]], axis=0).astype(BF16)
            for side, field in enumerate((low, value, high)):
                padded[side, 1 + line] = field
                turned[side, :, here] = field.T

    @pl.loop(0, 2)
    def _(step):
        pieces = [padded[oy, pl.ds(step * 4 + ox, 4)].reshape(512, 256) for ox in range(3) for oy in range(3)]
        here = pl.ds(pl.multiple_of(step * 512, 512), 512)
        pre[here, :] = levels(jnp.concatenate(pieces, axis=1), weights, (0, 1, 2), (0, 1, 2))

    copy.wait()


def chain_grads(at_ref, turned, ends, shifted, away, keep, chain):
    chan = 256
    core, mine, other = at_ref[0], at_ref[1 + 2 * chain], at_ref[2 + 2 * chain]
    for group in range(GROUPS[chain]):
        ox, oy = divmod(sum(GROUPS[:chain]) + group, 3)
        rows = []
        for half, quarter in ((core, mine), (1 - core, other)):
            for slot in range(4):
                here = pl.ds(pl.multiple_of(half * 128 + (quarter ^ slot) * 32, 32), 32)
                if ox == 0:
                    row = jnp.concatenate([ends[0, oy, here, :], turned[oy, here, 0:896]], axis=1)
                elif ox == 1:
                    row = turned[oy, here, :]
                else:
                    row = jnp.concatenate([turned[oy, here, 128:1024], ends[1, oy, here, :]], axis=1)
                rows.append(row)
        left = jnp.concatenate(rows, axis=0)
        for oz in range(3):
            part = jnp.dot(left, shifted[:, oz * chan : (oz + 1) * chan], preferred_element_type=F32)
            keep[:, :, group * 3 + oz] = part[:128].reshape(2, 2, 32, chan)
            away[:, :, group * 3 + oz] = part[128:].reshape(2, 2, 32, chan).astype(BF16)


def grads_kernel(at_ref, first, last, weights, pre, mgrad, turned, dpre, shifted, ends, away, keep):
    chan = 256
    lines = []
    for end, slab in ((0, first), (1, last)):
        line = slab[0:160, :].astype(F32)
        lines.append([line[8 + oy * 8 : 136 + oy * 8].astype(BF16) for oy in range(3)])
        for oy in range(3):
            ends[end, oy] = lines[end][oy].T
    for line in range(8):
        here = slice(line * 128, line * 128 + 128)
        value = pre[here, :]
        if line in (0, 7):
            end, ox = (0, 0) if line == 0 else (1, 2)
            value = value + levels(jnp.concatenate(lines[end], axis=1), weights, (0, 1, 2), (ox,))
        value = (mgrad[here, :].astype(F32) * dsilu(value)).astype(BF16)
        dpre[here, :] = value
        wide = value.astype(F32)
        shifted[here, 0:chan] = roll_cells(wide, -1).astype(BF16)
        shifted[here, chan : 2 * chan] = value
        shifted[here, 2 * chan : 3 * chan] = roll_cells(wide, 1).astype(BF16)
    chain_grads(at_ref, turned, ends, shifted, away, keep, 0)


def more_kernel(chain, at_ref, turned, ends, shifted, away, keep):
    chain_grads(at_ref, turned, ends, shifted, away, keep, chain)


def border_kernel(masked, before, after, first, last, weights, border, left):
    def cells(ref, start, stop):
        return ref[start:stop, :].astype(F32)

    def wide(line):
        near, at = slice(line * 8, line * 8 + 8), slice(line * 128, line * 128 + 128)
        return jnp.concatenate(
            [sides[0][1][near], sides[0][0][near], masked[at, :].astype(F32), sides[1][0][near], sides[1][1][near]], axis=0
        )

    sides = [[cells(ref, kind * 64, kind * 64 + 64) for kind in range(2)] for ref in (before, after)]
    ends = [[cells(ref, 0, 160), cells(ref, 160, 320)] for ref in (first, last)]
    edges = [[masked[x * 128 + y * 112 : x * 128 + y * 112 + 16, :].astype(F32) for x in range(8)] for y in range(2)]
    edge = [
        jnp.concatenate([v[:8] for v in edges[0]], axis=0),
        jnp.concatenate([v[8:] for v in edges[1]], axis=0),
    ]

    def column(index, body):
        at = slice(index * 8, index * 8 + 8)
        return jnp.concatenate([ends[0][0][at], body, ends[1][0][at]], axis=0)

    above = (ends[0][1], ends[0][0], wide(0))
    below = (wide(7), ends[1][0], ends[1][1])
    low = (column(0, sides[0][1]), column(1, sides[0][0]), column(2, edge[0]))
    high = (column(17, edge[1]), column(18, sides[1][0]), column(19, sides[1][1]))
    for ox in range(3):
        for oy in range(3):
            parts = [above[ox][oy * 8 : oy * 8 + 144], below[ox][oy * 8 : oy * 8 + 144]]
            parts += [low[oy][ox * 8 : ox * 8 + 64], high[oy][ox * 8 : ox * 8 + 64]]
            k = (ox * 3 + oy) * 256
            left[:, k : k + 256] = jnp.concatenate(parts, axis=0).astype(BF16)
    pre = None
    for oz in range(3):
        part = jnp.dot(left[...], weights[:, oz].reshape(2304, 256), preferred_element_type=F32)
        part = part if oz == 1 else roll_cells(part, 1 - oz)
        pre = part if pre is None else pre + part
    grad = [cells(first, 320, 464), cells(last, 320, 464), cells(before, 128, 192), cells(after, 128, 192)]
    border[...] = (jnp.concatenate(grad, axis=0) * dsilu(pre)).astype(BF16)


def input_kernel(part, occupied, dpre, border, weights, out, views):
    tile, chan = 512, 256
    lines = tile // 128

    line, start = ((0, 0), (5, 144))[part]
    value = border[start : start + 144, :].astype(F32)
    for side in range(3):
        views[side, line] = value[side * 8 : side * 8 + 128].astype(BF16)
    for pair in range(part, part + 3):
        low = border[288 + pair * 16 : 304 + pair * 16, :].astype(F32)
        high = border[352 + pair * 16 : 368 + pair * 16, :].astype(F32)
        for i in range(2):
            line = pair * 2 + i
            slot = line + 1 - part * 4
            if not 0 <= slot <= 5:
                continue
            value = dpre[line * 128 : line * 128 + 128, :]
            views[1, slot] = value
            value = value.astype(F32)
            views[0, slot] = jnp.concatenate([low[i * 8 : i * 8 + 8], value[:120]], axis=0).astype(BF16)
            views[2, slot] = jnp.concatenate([value[8:], high[i * 8 : i * 8 + 8]], axis=0).astype(BF16)

    pieces = []
    for ox in range(3):
        for oy in range(3):
            pieces.append(views[2 - oy, 2 - ox : 6 - ox].reshape(tile, chan))
    left = jnp.concatenate(pieces, axis=1)
    total = None
    for oz in range(3):
        right = jnp.concatenate([weights[k, oz] for k in range(9)], axis=1)
        field = lax.dot_general(left, right, (((1,), (1,)), ((), ())), preferred_element_type=F32)
        field = field if oz == 1 else roll_cells(field, oz - 1)
        total = field if total is None else total + field
    out[...] = (total * jnp.concatenate([line_mask(occupied, part)] * lines, axis=0)).astype(BF16)


def place_kernel(parts, at_ref, *refs):
    pieces, out, built, done = refs[: CHAINS * len(parts)], refs[-3], refs[-2], refs[-1]
    copies = []
    for index, (far, side) in enumerate(parts):
        half = at_ref[0] if side == 0 else 1 - at_ref[0]
        for chain in range(CHAINS):
            quarter = at_ref[1 + 2 * chain + side]
            row = pl.multiple_of(half * 128 + ((quarter // 2) ^ far) * 64, 64)
            for group in range(GROUPS[chain]):
                first = 3 * (sum(GROUPS[:chain]) + group)
                here = slice(first, first + 3)
                for slot in range(2):
                    start = pl.multiple_of(((quarter % 2) ^ slot) * 32, 32)
                    value = pieces[index * CHAINS + chain][slot, group * 3 : group * 3 + 3]
                    built[index, here, pl.ds(start, 32), :] = value.astype(F32)
                copy = pltpu.make_async_copy(
                    built.at[index, here], out.at[here, pl.ds(row, 64), :], done.at[len(copies)]
                )
                copy.start()
                copies.append(copy)
    for copy in copies:
        copy.wait()


VMEM = pl.BlockSpec(memory_space=pltpu.VMEM)
SMEM = pl.BlockSpec(memory_space=pltpu.SMEM)
HBM = pl.BlockSpec(memory_space=pltpu.HBM)


def shape(*dims, dtype=BF16):
    return jax.ShapeDtypeStruct(dims, dtype)


def chain_shapes(chain):
    dims = (2, 2, 3 * GROUPS[chain], 32, 256)
    return shape(*dims), shape(*dims, dtype=F32)


def kernel(body, outs, specs, args, flops, scratch=(), out_specs=None, aliases=None, nbytes=6_000_000, room=20):
    return pl.pallas_call(
        body,
        out_shape=outs,
        in_specs=specs,
        out_specs=out_specs if out_specs is not None else jax.tree.map(lambda _: VMEM, outs),
        scratch_shapes=scratch,
        input_output_aliases=aliases or {},
        compiler_params=pltpu.CompilerParams(vmem_limit_bytes=room * 2**20),
        cost_estimate=pl.CostEstimate(flops=flops, bytes_accessed=nbytes, transcendentals=0),
    )(*args)


def put_in_place(parts, at, pieces, out=None):
    more = () if out is None else (out,)
    return kernel(
        functools.partial(place_kernel, parts),
        shape(27, 256, 256, dtype=F32),
        [SMEM] + [VMEM] * len(pieces) + [HBM] * len(more),
        (at, *pieces, *more),
        0,
        [pltpu.VMEM((len(parts), 27, 64, 256), F32), pltpu.SemaphoreType.DMA((9 * len(parts),))],
        HBM,
        {1 + len(pieces): 0} if more else {},
        nbytes=10_000_000,
    )


CONV = 3_623_878_656


def local(features, grad_out, weights, occupied):
    at = where_am_i()
    cells, chan = 1024, 256
    packed = weights.reshape(9, 3, chan, chan)
    occupied = jnp.transpose(occupied, (0, 2, 1))
    mask = kernel(mask_kernel, shape(cells, chan), [SMEM], (occupied,), 0, nbytes=500_000).reshape(features.shape)
    masked, mgrad = features * mask, grad_out * mask
    head, tail = (
        jnp.concatenate([v.reshape(64, chan) for v in (masked[:, a], masked[:, b], mgrad[:, a])]) for a, b in ((0, 1), (15, 14))
    )
    masked, mgrad = masked.reshape(cells, chan), mgrad.reshape(cells, chan)
    before, after = neighbours("gy", head, tail)
    first, last_line = neighbours("gx", *slabs(masked, mgrad, before, after))
    pre, turned, held = kernel(
        inner_kernel,
        (shape(cells, chan, dtype=F32), shape(3, chan, cells), shape(9, 3, chan, chan)),
        [VMEM] * 4,
        (masked, before, after, packed),
        CONV,
        [pltpu.VMEM((3, 10, 128, chan), BF16), pltpu.SemaphoreType.DMA],
    )
    dpre, shifted, ends, away, keep = kernel(
        grads_kernel,
        (shape(cells, chan), shape(cells, 3 * chan), shape(2, 3, chan, 128), *chain_shapes(0)),
        [SMEM] + [VMEM] * 6,
        (at, first, last_line, held, pre, mgrad, turned),
        CONV // 2,
    )
    got, keeps, tie = [], [keep], lax.optimization_barrier
    for chain in range(CHAINS):
        got.append(send(away, core_pairs()))
        if chain < CHAINS - 1:
            away, keep = kernel(
                functools.partial(more_kernel, chain + 1),
                chain_shapes(chain + 1),
                [SMEM] + [VMEM] * 3,
                (at, turned, ends, shifted),
                CONV // 3,
            )
            keeps.append(keep)
            away, got[chain] = tie((away, got[chain]))
    halves = []
    sums = [keep + g.astype(F32) for keep, g in zip(keeps, got)]
    for step in range(6):
        for chain in range(CHAINS):
            give = sums[chain][1].astype(BF16) if step < 2 else sums[chain]
            got[chain] = send(give, step_pairs(chain, step))
        if step == 3:
            border = kernel(
                border_kernel,
                shape(416, chan),
                [VMEM] * 6,
                (masked, before, after, first, last_line, packed),
                CONV // 2,
                [pltpu.VMEM((416, 9 * chan), BF16)],
            )
            got[0], border = tie((got[0], border))
        if step > 3:
            half = kernel(
                functools.partial(input_kernel, step - 4),
                shape(cells // 2, chan),
                [SMEM, VMEM, VMEM, VMEM],
                (occupied, dpre, border, packed),
                CONV // 2,
                [pltpu.VMEM((3, 6, 128, chan), BF16)],
            )
            got[0], half = tie((got[0], half))
            halves.append(half)
        for chain in range(CHAINS):
            if chain == 0 and step:
                got[0], sums[-1] = tie((got[0], sums[-1]))
            own = sums[chain][0] if step < 2 else sums[chain]
            total = own.astype(F32) + got[chain].astype(F32)
            sums[chain] = total if step < 1 else total.astype(BF16)
    for chain in range(CHAINS):
        got[chain] = send(sums[chain], step_pairs(chain, 1))
    grad_features = jnp.concatenate(halves)
    got[0], sums[-1], grad_features = tie((got[0], sums[-1], grad_features))
    nears, fars = [], []
    for chain in range(CHAINS):
        nears.append(jnp.stack([sums[chain], got[chain]]))
        fars.append(send(nears[chain], step_pairs(chain, 0)))
    out = put_in_place(((0, 0),), at, nears)
    fars[0], out, *nears = tie((fars[0], out, *nears))
    other_nears = [send(near, core_pairs()) for near in nears]
    others = [send(far, core_pairs()) for far in fars]
    out = put_in_place(((1, 0), (0, 1)), at, fars + other_nears, out)
    out = put_in_place(((1, 1),), at, others, out)
    return grad_features.reshape(features.shape), out


def solution(mesh):
    return jax.shard_map(
        local,
        mesh=mesh,
        in_specs=(P("gx", "gy", None, None), P("gx", "gy", None, None), P(), P("gx", "gy", None)),
        out_specs=(P("gx", "gy", None, None), P()),
        check_vma=False,
    )
```

```python
import functools

import jax
import jax.numpy as jnp
from jax import lax
from jax.experimental import pallas as pl
from jax.experimental.pallas import tpu as pltpu
from jax.sharding import PartitionSpec as P

AXES = ("gx", "gy")
F32, BF16 = jnp.float32, jnp.bfloat16
COUNT = 128
FIRSTS = ((0, 4), (3, 1))
ORDERS = tuple(
    tuple(tuple((first + step) % 6 for step in range(6)) for first in firsts) for firsts in FIRSTS
)
GROUPS = (5, 4)
CHAINS = len(GROUPS)


def place(index):
    gx, gy = index // 8, index % 8
    return (gx // 2) % 4, (gx // 8) * 2 + gy // 4, gy % 4, gx % 2


def index_of(x, y, z, core):
    return ((y // 2) * 8 + x * 2 + core) * 8 + (y % 2) * 4 + z


def step_pairs(chain, step):
    pairs = []
    for i in range(COUNT):
        *at, core = place(i)
        dim = ORDERS[chain][core][step]
        at[dim % 3] = at[dim % 3] ^ 1 if dim < 3 else 3 - at[dim % 3]
        pairs.append((i, index_of(*at, core)))
    return pairs


def core_pairs():
    return [(i, index_of(*place(i)[:3], 1 - place(i)[3])) for i in range(COUNT)]


def send(array, pairs):
    return lax.ppermute(array, AXES, pairs)


def where_am_i():
    gx, gy = lax.axis_index("gx"), lax.axis_index("gy")
    core = gx % 2
    at = [(gx // 2) % 4, (gx // 8) * 2 + gy // 4, gy % 4]
    side = [(v % 2) ^ (v // 2) for v in at] + [v // 2 for v in at]
    found = [core]
    for chain in range(CHAINS):
        quarters = [side[order[0]] * 2 + side[order[1]] for order in ORDERS[chain]]
        found.append(jnp.where(core == 0, quarters[0], quarters[1]))
        found.append(jnp.where(core == 0, quarters[1], quarters[0]))
    return jnp.stack(found).astype(jnp.int32)


def pair_swap(axis, first, array):
    count = lax.axis_size(axis)
    pairs = [(i, i + 1) for i in range(first, count - 1, 2)]
    return lax.ppermute(array, axis, pairs + [(b, a) for a, b in pairs])


def neighbours(axis, head, tail):
    even = lax.axis_index(axis) % 2 == 0
    one = pair_swap(axis, 0, jnp.where(even, tail, head))
    two = pair_swap(axis, 1, jnp.where(even, head, tail))
    return jnp.where(even, two, one), jnp.where(even, one, two)


def slabs(masked, mgrad, before, after):
    beside = [(b, a) for b, a in zip(before.reshape(3, 8, 8, 256), after.reshape(3, 8, 8, 256))]
    found = []
    for near, next_one in ((0, 1), (7, 6)):
        parts = []
        for line in (near, next_one):
            at = slice(line * 128, line * 128 + 128)
            parts += [beside[1][0][line], beside[0][0][line], masked[at], beside[0][1][line], beside[1][1][line]]
        at = slice(near * 128, near * 128 + 128)
        parts += [beside[2][0][near], mgrad[at], beside[2][1][near]]
        found.append(jnp.concatenate(parts))
    return found


def roll_cells(field, step):
    cells, chan = field.shape
    tall = field.reshape(cells // 8, 8, chan)
    level = lax.broadcasted_iota(jnp.int32, tall.shape, 1)
    moved = pltpu.roll(tall, step % 8, 1)
    kept = jnp.where((level >= step) & (level < 8 + step), moved, 0.0)
    return kept.reshape(cells, chan)


def dsilu(pre):
    sig = jax.nn.sigmoid(pre)
    return sig * (1.0 + pre * (1.0 - sig))


def brick_mask(occupied, bx, by):
    level = lax.broadcasted_iota(jnp.int32, (8, 256), 0)
    return jnp.where(level < 4, occupied[bx, 0, by], occupied[bx, 1, by]).astype(F32)


def line_mask(occupied, bx):
    return jnp.concatenate([brick_mask(occupied, bx, by) for by in range(4) for _ in range(4)], axis=0)


def mask_kernel(occupied, mask):
    for bx in range(2):
        lines = line_mask(occupied, bx).astype(BF16)
        for line in range(bx * 4, bx * 4 + 4):
            mask[line * 128 : line * 128 + 128, :] = lines


def levels(left, weights, oy_list, ox_list):
    pre = None
    for oz in range(3):
        right = jnp.concatenate([weights[ox * 3 + oy, oz] for ox in ox_list for oy in oy_list], axis=0)
        part = jnp.dot(left, right, preferred_element_type=F32)
        part = part if oz == 1 else roll_cells(part, 1 - oz)
        pre = part if pre is None else pre + part
    return pre


def inner_kernel(masked, before, after, weights, pre, turned, held, padded, copied):
    copy = pltpu.make_async_copy(weights, held, copied)
    copy.start()
    for side in range(3):
        padded[side, 0] = jnp.zeros((128, 256), BF16)
        padded[side, 9] = jnp.zeros((128, 256), BF16)
    for pair in range(4):
        left = before[pair * 16 : pair * 16 + 16, :].astype(F32)
        right = after[pair * 16 : pair * 16 + 16, :].astype(F32)
        for i in range(2):
            line = pair * 2 + i
            here = slice(line * 128, line * 128 + 128)
            value = masked[here, :]
            wide = value.astype(F32)
            low = jnp.concatenate([left[i * 8 : i * 8 + 8], wide[:120]], axis=0).astype(BF16)
            high = jnp.concatenate([wide[8:], right[i * 8 : i * 8 + 8]], axis=0).astype(BF16)
            for side, field in enumerate((low, value, high)):
                padded[side, 1 + line] = field
                turned[side, :, here] = field.T

    @pl.loop(0, 2)
    def _(step):
        pieces = [padded[oy, pl.ds(step * 4 + ox, 4)].reshape(512, 256) for ox in range(3) for oy in range(3)]
        here = pl.ds(pl.multiple_of(step * 512, 512), 512)
        pre[here, :] = levels(jnp.concatenate(pieces, axis=1), weights, (0, 1, 2), (0, 1, 2))

    copy.wait()


def chain_grads(at_ref, turned, ends, shifted, away, keep, chain):
    chan = 256
    core, mine, other = at_ref[0], at_ref[1 + 2 * chain], at_ref[2 + 2 * chain]
    for group in range(GROUPS[chain]):
        ox, oy = divmod(sum(GROUPS[:chain]) + group, 3)
        rows = []
        for half, quarter in ((core, mine), (1 - core, other)):
            for slot in range(4):
                here = pl.ds(pl.multiple_of(half * 128 + (quarter ^ slot) * 32, 32), 32)
                if ox == 0:
                    row = jnp.concatenate([ends[0, oy, here, :], turned[oy, here, 0:896]], axis=1)
                elif ox == 1:
                    row = turned[oy, here, :]
                else:
                    row = jnp.concatenate([turned[oy, here, 128:1024], ends[1, oy, here, :]], axis=1)
                rows.append(row)
        left = jnp.concatenate(rows, axis=0)
        for oz in range(3):
            part = jnp.dot(left, shifted[:, oz * chan : (oz + 1) * chan], preferred_element_type=F32)
            keep[:, :, group * 3 + oz] = part[:128].reshape(2, 2, 32, chan)
            away[:, :, group * 3 + oz] = part[128:].reshape(2, 2, 32, chan).astype(BF16)


def grads_kernel(at_ref, first, last, weights, pre, mgrad, turned, dpre, shifted, ends, away, keep):
    chan = 256
    lines = []
    for end, slab in ((0, first), (1, last)):
        line = slab[0:160, :].astype(F32)
        lines.append([line[8 + oy * 8 : 136 + oy * 8].astype(BF16) for oy in range(3)])
        for oy in range(3):
            ends[end, oy] = lines[end][oy].T
    for line in range(8):
        here = slice(line * 128, line * 128 + 128)
        value = pre[here, :]
        if line in (0, 7):
            end, ox = (0, 0) if line == 0 else (1, 2)
            value = value + levels(jnp.concatenate(lines[end], axis=1), weights, (0, 1, 2), (ox,))
        value = (mgrad[here, :].astype(F32) * dsilu(value)).astype(BF16)
        dpre[here, :] = value
        wide = value.astype(F32)
        shifted[here, 0:chan] = roll_cells(wide, -1).astype(BF16)
        shifted[here, chan : 2 * chan] = value
        shifted[here, 2 * chan : 3 * chan] = roll_cells(wide, 1).astype(BF16)
    chain_grads(at_ref, turned, ends, shifted, away, keep, 0)


def more_kernel(chain, at_ref, turned, ends, shifted, away, keep):
    chain_grads(at_ref, turned, ends, shifted, away, keep, chain)


def border_kernel(masked, before, after, first, last, weights, border, left):
    def cells(ref, start, stop):
        return ref[start:stop, :].astype(F32)

    def wide(line):
        near, at = slice(line * 8, line * 8 + 8), slice(line * 128, line * 128 + 128)
        return jnp.concatenate(
            [sides[0][1][near], sides[0][0][near], masked[at, :].astype(F32), sides[1][0][near], sides[1][1][near]], axis=0
        )

    sides = [[cells(ref, kind * 64, kind * 64 + 64) for kind in range(2)] for ref in (before, after)]
    ends = [[cells(ref, 0, 160), cells(ref, 160, 320)] for ref in (first, last)]
    edges = [[masked[x * 128 + y * 112 : x * 128 + y * 112 + 16, :].astype(F32) for x in range(8)] for y in range(2)]
    edge = [
        jnp.concatenate([v[:8] for v in edges[0]], axis=0),
        jnp.concatenate([v[8:] for v in edges[1]], axis=0),
    ]

    def column(index, body):
        at = slice(index * 8, index * 8 + 8)
        return jnp.concatenate([ends[0][0][at], body, ends[1][0][at]], axis=0)

    above = (ends[0][1], ends[0][0], wide(0))
    below = (wide(7), ends[1][0], ends[1][1])
    low = (column(0, sides[0][1]), column(1, sides[0][0]), column(2, edge[0]))
    high = (column(17, edge[1]), column(18, sides[1][0]), column(19, sides[1][1]))
    for ox in range(3):
        for oy in range(3):
            parts = [above[ox][oy * 8 : oy * 8 + 144], below[ox][oy * 8 : oy * 8 + 144]]
            parts += [low[oy][ox * 8 : ox * 8 + 64], high[oy][ox * 8 : ox * 8 + 64]]
            k = (ox * 3 + oy) * 256
            left[:, k : k + 256] = jnp.concatenate(parts, axis=0).astype(BF16)
    pre = None
    for oz in range(3):
        part = jnp.dot(left[...], weights[:, oz].reshape(2304, 256), preferred_element_type=F32)
        part = part if oz == 1 else roll_cells(part, 1 - oz)
        pre = part if pre is None else pre + part
    grad = [cells(first, 320, 464), cells(last, 320, 464), cells(before, 128, 192), cells(after, 128, 192)]
    border[...] = (jnp.concatenate(grad, axis=0) * dsilu(pre)).astype(BF16)


def input_kernel(part, occupied, dpre, border, weights, out, views):
    tile, chan = 512, 256
    lines = tile // 128

    line, start = ((0, 0), (5, 144))[part]
    value = border[start : start + 144, :].astype(F32)
    for side in range(3):
        views[side, line] = value[side * 8 : side * 8 + 128].astype(BF16)
    for pair in range(part, part + 3):
        low = border[288 + pair * 16 : 304 + pair * 16, :].astype(F32)
        high = border[352 + pair * 16 : 368 + pair * 16, :].astype(F32)
        for i in range(2):
            line = pair * 2 + i
            slot = line + 1 - part * 4
            if not 0 <= slot <= 5:
                continue
            value = dpre[line * 128 : line * 128 + 128, :]
            views[1, slot] = value
            value = value.astype(F32)
            views[0, slot] = jnp.concatenate([low[i * 8 : i * 8 + 8], value[:120]], axis=0).astype(BF16)
            views[2, slot] = jnp.concatenate([value[8:], high[i * 8 : i * 8 + 8]], axis=0).astype(BF16)

    pieces = []
    for ox in range(3):
        for oy in range(3):
            pieces.append(views[2 - oy, 2 - ox : 6 - ox].reshape(tile, chan))
    left = jnp.concatenate(pieces, axis=1)
    total = None
    for oz in range(3):
        right = jnp.concatenate([weights[k, oz] for k in range(9)], axis=1)
        field = lax.dot_general(left, right, (((1,), (1,)), ((), ())), preferred_element_type=F32)
        field = field if oz == 1 else roll_cells(field, oz - 1)
        total = field if total is None else total + field
    out[...] = (total * jnp.concatenate([line_mask(occupied, part)] * lines, axis=0)).astype(BF16)


def place_kernel(parts, at_ref, *refs):
    pieces, out, built, done = refs[: CHAINS * len(parts)], refs[-3], refs[-2], refs[-1]
    copies = []
    for index, (far, side) in enumerate(parts):
        half = at_ref[0] if side == 0 else 1 - at_ref[0]
        for chain in range(CHAINS):
            quarter = at_ref[1 + 2 * chain + side]
            row = pl.multiple_of(half * 128 + ((quarter // 2) ^ far) * 64, 64)
            for group in range(GROUPS[chain]):
                first = 3 * (sum(GROUPS[:chain]) + group)
                here = slice(first, first + 3)
                for slot in range(2):
                    start = pl.multiple_of(((quarter % 2) ^ slot) * 32, 32)
                    value = pieces[index * CHAINS + chain][slot, group * 3 : group * 3 + 3]
                    built[index, here, pl.ds(start, 32), :] = value.astype(F32)
                copy = pltpu.make_async_copy(
                    built.at[index, here], out.at[here, pl.ds(row, 64), :], done.at[len(copies)]
                )
                copy.start()
                copies.append(copy)
    for copy in copies:
        copy.wait()


VMEM = pl.BlockSpec(memory_space=pltpu.VMEM)
SMEM = pl.BlockSpec(memory_space=pltpu.SMEM)
HBM = pl.BlockSpec(memory_space=pltpu.HBM)


def shape(*dims, dtype=BF16):
    return jax.ShapeDtypeStruct(dims, dtype)


def chain_shapes(chain):
    dims = (2, 2, 3 * GROUPS[chain], 32, 256)
    return shape(*dims), shape(*dims, dtype=F32)


def kernel(body, outs, specs, args, flops, scratch=(), out_specs=None, aliases=None, nbytes=6_000_000, room=20):
    return pl.pallas_call(
        body,
        out_shape=outs,
        in_specs=specs,
        out_specs=out_specs if out_specs is not None else jax.tree.map(lambda _: VMEM, outs),
        scratch_shapes=scratch,
        input_output_aliases=aliases or {},
        compiler_params=pltpu.CompilerParams(vmem_limit_bytes=room * 2**20),
        cost_estimate=pl.CostEstimate(flops=flops, bytes_accessed=nbytes, transcendentals=0),
    )(*args)


def put_in_place(parts, at, pieces, out=None):
    more = () if out is None else (out,)
    return kernel(
        functools.partial(place_kernel, parts),
        shape(27, 256, 256, dtype=F32),
        [SMEM] + [VMEM] * len(pieces) + [HBM] * len(more),
        (at, *pieces, *more),
        0,
        [pltpu.VMEM((len(parts), 27, 64, 256), F32), pltpu.SemaphoreType.DMA((9 * len(parts),))],
        HBM,
        {1 + len(pieces): 0} if more else {},
        nbytes=10_000_000,
    )


CONV = 3_623_878_656


def local(features, grad_out, weights, occupied):
    at = where_am_i()
    cells, chan = 1024, 256
    packed = weights.reshape(9, 3, chan, chan)
    occupied = jnp.transpose(occupied, (0, 2, 1))
    mask = kernel(mask_kernel, shape(cells, chan), [SMEM], (occupied,), 0, nbytes=500_000).reshape(features.shape)
    masked, mgrad = features * mask, grad_out * mask
    head, tail = (
        jnp.concatenate([v.reshape(64, chan) for v in (masked[:, a], masked[:, b], mgrad[:, a])]) for a, b in ((0, 1), (15, 14))
    )
    masked, mgrad = masked.reshape(cells, chan), mgrad.reshape(cells, chan)
    before, after = neighbours("gy", head, tail)
    first, last_line = neighbours("gx", *slabs(masked, mgrad, before, after))
    pre, turned, held = kernel(
        inner_kernel,
        (shape(cells, chan, dtype=F32), shape(3, chan, cells), shape(9, 3, chan, chan)),
        [VMEM] * 4,
        (masked, before, after, packed),
        CONV,
        [pltpu.VMEM((3, 10, 128, chan), BF16), pltpu.SemaphoreType.DMA],
    )
    dpre, shifted, ends, away, keep = kernel(
        grads_kernel,
        (shape(cells, chan), shape(cells, 3 * chan), shape(2, 3, chan, 128), *chain_shapes(0)),
        [SMEM] + [VMEM] * 6,
        (at, first, last_line, held, pre, mgrad, turned),
        CONV // 2,
    )
    got, keeps, tie = [], [keep], lax.optimization_barrier
    for chain in range(CHAINS):
        got.append(send(away, core_pairs()))
        if chain < CHAINS - 1:
            away, keep = kernel(
                functools.partial(more_kernel, chain + 1),
                chain_shapes(chain + 1),
                [SMEM] + [VMEM] * 3,
                (at, turned, ends, shifted),
                CONV // 3,
            )
            keeps.append(keep)
            away, got[chain] = tie((away, got[chain]))
    halves = []
    sums = [keep + g.astype(F32) for keep, g in zip(keeps, got)]
    for step in range(6):
        for chain in range(CHAINS):
            give = sums[chain][1].astype(BF16) if step < 2 else sums[chain]
            got[chain] = send(give, step_pairs(chain, step))
        if step == 3:
            border = kernel(
                border_kernel,
                shape(416, chan),
                [VMEM] * 6,
                (masked, before, after, first, last_line, packed),
                CONV // 2,
                [pltpu.VMEM((416, 9 * chan), BF16)],
            )
            got[0], border = tie((got[0], border))
        if step > 3:
            half = kernel(
                functools.partial(input_kernel, step - 4),
                shape(cells // 2, chan),
                [SMEM, VMEM, VMEM, VMEM],
                (occupied, dpre, border, packed),
                CONV // 2,
                [pltpu.VMEM((3, 6, 128, chan), BF16)],
            )
            got[0], half = tie((got[0], half))
            halves.append(half)
        for chain in range(CHAINS):
            if chain == 0 and step:
                got[0], sums[-1] = tie((got[0], sums[-1]))
            own = sums[chain][0] if step < 2 else sums[chain]
            total = own.astype(F32) + got[chain].astype(F32)
            sums[chain] = total if step < 1 else total.astype(BF16)
    for chain in range(CHAINS):
        got[chain] = send(sums[chain], step_pairs(chain, 1))
    grad_features = jnp.concatenate(halves)
    got[0], sums[-1], grad_features = tie((got[0], sums[-1], grad_features))
    nears, fars = [], []
    for chain in range(CHAINS):
        nears.append(jnp.stack([sums[chain], got[chain]]))
        fars.append(send(nears[chain], step_pairs(chain, 0)))
    out = put_in_place(((0, 0),), at, nears)
    fars[0], out, *nears = tie((fars[0], out, *nears))
    other_nears = [send(near, core_pairs()) for near in nears]
    others = [send(far, core_pairs()) for far in fars]
    out = put_in_place(((1, 0), (0, 1)), at, fars + other_nears, out)
    out = put_in_place(((1, 1),), at, others, out)
    return grad_features.reshape(features.shape), out


def solution(mesh):
    return jax.shard_map(
        local,
        mesh=mesh,
        in_specs=(P("gx", "gy", None, None), P("gx", "gy", None, None), P(), P("gx", "gy", None)),
        out_specs=(P("gx", "gy", None, None), P()),
        check_vma=False,
    )
```
